32 devices in a mesh: groups: 2 (over x), dp: 16 (over z, y, core).
Axes of the slice: x: 2, y: 2, z: 4, core: 2. Of those that a mesh axis runs over, the one named last changes fastest.
Arguments:
- test_feats: bfloat16 [1024, 8192], P('groups', 'dp'), parts along dimension 0, may hold values from -6 to 6
- precond: bfloat16 [8192, 8192], P('dp'), may hold values from -0.0625 to 0.0625
- train_feats: bfloat16 [16384, 8192], P(('groups', 'dp')), parts along dimension 0, may hold values from -6 to 6
- train_prob: float32 [16384], P(('groups', 'dp')), parts along dimension 0, may hold values from 0.05 to 0.95
Outputs:
- scores: float32 [16384, 512], P(('groups', 'dp')), parts along dimension 0
The draws below stay inside these ranges and needn't reach their ends.
There are 2 independent parts, one for each index of `groups`. The reference program is written for one: setup_inputs(seed, part) draws one part's arguments, and reference() takes and returns one part's arrays. A program takes and returns all parts, laid end to end along the dimension named above; an argument that names none is the same for every part. Nothing has to cross between parts.
All inputs are finite; a program needn't handle non-finite values.
Results may differ from the reference program's by a relative error of at most 0.0029.
Values may be sent and summed in bfloat16 or wider, within the bound.
A program may use at most 128 MiB of HBM per device.

```python
import jax
import jax.numpy as jnp
from jax import lax

FEATURES = 8192
TEST = 512
TRAIN = 8192


def spiked(entries, rng, source, target, shards_of, factor):
    owner, partner = [(jnp.arange(entries.shape[axis_at]) // (entries.shape[axis_at] // shards_of)).reshape([-1 if axis == axis_at else 1 for axis in range(entries.ndim)]) for axis_at in (source, target)]
    chosen = jax.random.permutation(rng, shards_of)[partner]
    strong = (owner == chosen) | (owner == (partner + shards_of // 2) % shards_of)
    return jnp.where(strong, factor * entries, entries)


def steps_of(key, shape, shards, least, top_value):
    level = 1.0
    for axis_at, shards_of in shards:
        draws = jax.random.uniform(jax.random.fold_in(jax.random.fold_in(key, 6), axis_at), (shards_of,), jnp.float32, least / len(shards), top_value / len(shards))
        level = level * jnp.repeat(jnp.exp(draws), shape[axis_at] // shards_of).reshape((-1,) + (1,) * (len(shape) - 1 - axis_at))
    return level


def gaussian(own_key, extent, width, reach, shards=(), kind=jnp.bfloat16):
    factor_of = steps_of(own_key, extent, shards, -0.22, 0.18) if shards else 1.0
    result = jax.random.normal(own_key, extent, jnp.float32) * width * factor_of
    return jnp.minimum(jnp.maximum(result, -reach), reach).astype(kind)


def gaussian_with(stream_key, extent, deviation, limit, split, heavy, dtype=jnp.bfloat16):
    drawn = deviation * jax.random.normal(stream_key, extent, jnp.float32)
    if split:
        drawn = drawn * steps_of(stream_key, extent, split, -0.22, 0.18)
    return jnp.clip(spiked(drawn, jax.random.fold_in(stream_key, 3), *heavy), -limit, limit).astype(dtype)


def setup_inputs(seed: int = 0, part: int = 0) -> dict:
    seeds = jax.random.split(jax.random.key(seed), 5)
    part_splits = jax.random.split(jax.random.fold_in(seeds[4], part), 5)
    test_feats = gaussian_with(part_splits[0], (TEST, FEATURES), 1.0, 6.0, ((1, 16),), (1, 0, 16, 2.0))
    precond = gaussian(seeds[1], (FEATURES, FEATURES), FEATURES ** -0.5, 0.0625, ((0, 16),))
    train_feats = gaussian(part_splits[2], (TRAIN, FEATURES), 1.0, 6.0, ((0, 16),))
    train_prob = jnp.clip(0.05 + 0.9 * jax.random.uniform(part_splits[3], (TRAIN,), jnp.float32) ** steps_of(part_splits[3], (TRAIN,), ((0, 16),), -0.2, 0.2), 0.05, 0.95)
    return dict(test_feats=test_feats, precond=precond, train_feats=train_feats, train_prob=train_prob)


def reference(test_feats, precond, train_feats, train_prob):
    test_pre = jnp.dot(test_feats, precond, preferred_element_type=jnp.float32).astype(jnp.bfloat16)
    test_wide = test_pre.astype(jnp.float32)
    blocks = train_feats.reshape(TRAIN // 512 if TRAIN % 512 == 0 else TRAIN, -1, FEATURES)

    def one_block(rows):
        return jnp.dot(rows.astype(jnp.float32), test_wide.T)

    raw_scores = lax.map(one_block, blocks).reshape(TRAIN, TEST)
    return raw_scores * (1.0 - train_prob)[:, None]
```

```python
import functools

import jax
import jax.numpy as jnp
from jax import lax
from jax.experimental import pallas as pl
from jax.experimental.pallas import tpu as pltpu
from jax.sharding import PartitionSpec as P

MESH = pl.DeviceIdType.MESH
F32, BF16 = jnp.float32, jnp.bfloat16


def narrow_hops(chips):
    count = 0
    while (count + 1) * (count + 2) <= 0.8 * chips and count + 1 < chips // 2:
        count += 1
    return count


def kernel(
    chips, folded, narrow,
    test_ref, precond_hbm, train_hbm, out_ref,
    test_other, own_p, other_p, train, part, mine,
    send16, send32, recv16, recv32, gathered,
    test_sems, own_sems, other_sems, train_sem,
    ring_sems, spread_sems, pair_sems,
):
    half = chips // 2
    tests, depth = test_ref.shape
    rows = tests // 2
    feats = own_p.shape[2]
    index = lax.axis_index("dp")
    core = index % 2
    chip = index // 2
    if folded:
        pos = chip // 2 + (chip % 2) * (chips - 1 - 2 * (chip // 2))
    else:
        pos = chip

    def device(place):
        place = (place + chips) % chips
        if folded:
            side = place // half
            place = 2 * (place + side * (chips - 1 - 2 * place)) + side
        return {"dp": place * 2 + core}

    pair = {"dp": chip * 2 + 1 - core}
    towards = (device(pos + 1), device(pos - 1))

    def columns(offset, which):
        block = ((pos + offset + chips) % chips) * 2 + which
        return pl.ds(pl.multiple_of(block * feats, feats), feats)

    order = [half]
    for distance in range(half - 1, 0, -1):
        order += [distance, -distance]
    order.append(0)

    barrier = pltpu.get_barrier_semaphore()
    train_copy = pltpu.make_async_copy(train_hbm, train, train_sem)
    own_copies = [
        pltpu.make_async_copy(
            precond_hbm.at[:, columns(offset, core)], own_p.at[at], own_sems.at[at]
        )
        for at, offset in enumerate(order)
    ]
    for copy in own_copies:
        copy.start()
    for other in (pair, *towards):
        pl.semaphore_signal(barrier, inc=1, device_id=other, device_id_type=MESH)
    pl.semaphore_wait(barrier, 3)

    def remote(src, dst, sems, where):
        return pltpu.make_async_remote_copy(
            src_ref=src, dst_ref=dst,
            send_sem=sems.at[(0, *where)], recv_sem=sems.at[(1, *where)],
            device_id=where_to[0], device_id_type=MESH,
        )

    where_to = [pair]
    sent = []
    test_copy = remote(test_ref, test_other, test_sems, (0,))
    test_copy.start()
    sent.append(test_copy)
    other_copies = []
    for at, offset in enumerate(order):
        copy = remote(
            precond_hbm.at[:, columns(offset, 1 - core)], other_p.at[at], other_sems, (at,)
        )
        copy.start()
        sent.append(copy)
        other_copies.append(copy)
    train_copy.start()

    tile = min(rows, 256)

    def partial_sum(offset, target):
        at = order.index(offset)
        own_copies[at].wait()
        if at == 0:
            test_copy.wait_recv()
        other_copies[at].wait_recv()

        @pl.loop(0, tests // tile)
        def _(step):
            here = pl.ds(pl.multiple_of(step * tile, tile), tile)
            target[here, :] = jnp.dot(
                test_ref[here, :], own_p[at], preferred_element_type=F32
            ) + jnp.dot(test_other[here, :], other_p[at], preferred_element_type=F32)

    def slot(way, which, step):
        count = step + 1 if way == which else step
        if count <= narrow:
            return send16.at[way, which, step], recv16.at[way, which, step]
        return send32.at[way, which, step - narrow], recv32.at[way, which, step - narrow]

    ring = {}
    sign = (1, -1)
    partial_sum(half, part.at[0])
    for step in range(half):
        if step > 0:
            for way in (0, 1):
                partial_sum(sign[way] * (half - step), part.at[way])
        for leg in (0, 1):
            for way in (0, 1):
                which = way if leg == 0 else 1 - way
                if step == 0 and leg == 1:
                    continue
                source, target = slot(way, which, step)
                value = part[0 if step == 0 else way, pl.ds(which * rows, rows), :]
                if (way, which, step - 1) in ring:
                    ring[way, which, step - 1].wait_recv()
                    value = value + slot(way, which, step - 1)[1][...].astype(F32)
                source[...] = value.astype(source.dtype)
                where_to[0] = towards[way]
                copy = remote(source, target, ring_sems, (way, which, step))
                copy.start()
                sent.append(copy)
                ring[way, which, step] = copy
    partial_sum(0, mine)

    def place(offset, which):
        return ((pos + offset + chips) % chips) * 2 + which

    def span(which):
        return pl.ds(which * rows, rows)

    spread, paired = {}, {}

    def forward(way, which, step):
        block = gathered.at[place(-sign[way] * step, core), span(which)]
        where_to[0] = towards[way]
        copy = remote(block, block, spread_sems, (way, which, step))
        copy.start()
        sent.append(copy)
        spread[way, which, step] = copy

    def hand_over(way, which, step):
        block = gathered.at[place(-sign[way] * step, core), span(which)]
        where_to[0] = pair
        copy = remote(block, block, pair_sems, (way, which, step))
        copy.start()
        sent.append(copy)
        paired[way, which, step] = copy

    out_ref[...] = jnp.zeros_like(out_ref)

    def fold(offset, owner, which):
        block = place(offset, owner)
        cols = pl.ds(pl.multiple_of(block * feats, feats), feats)
        size = min(256, out_ref.shape[0])

        @pl.loop(0, out_ref.shape[0] // size)
        def _(step):
            here = pl.ds(pl.multiple_of(step * size, size), size)
            out_ref[here, which * rows:(which + 1) * rows] += lax.dot_general(
                train[here, cols], gathered[block, span(which), :],
                (((1,), (1,)), ((), ())), preferred_element_type=F32,
            )

    train_copy.wait()
    ready = []
    for which in (0, 1):
        total = mine[span(which), :]
        for way in (0, 1):
            ring[way, which, half - 1].wait_recv()
            total = total + slot(way, which, half - 1)[1][...].astype(F32)
        gathered[place(0, core), span(which), :] = total.astype(BF16)
        for way in (0, 1):
            if half > 1 or way == which:
                forward(way, which, 0)
        hand_over(0, which, 0)
        ready += [(0, core, which, None), (0, 1 - core, which, (0, which, 0))]

    def drain(limit):
        while len(ready) > limit:
            offset, owner, which, key = ready.pop(0)
            if key is not None:
                paired[key].wait_recv()
            fold(offset, owner, which)

    for step in range(1, half + 1):
        for which in (0, 1):
            for way in (0, 1):
                if (way, which, step - 1) not in spread:
                    continue
                spread[way, which, step - 1].wait_recv()
                if step < half and (step + 1 < half or way == which):
                    forward(way, which, step)
                hand_over(way, which, step)
                offset = -sign[way] * step
                ready += [
                    (offset, core, which, None), (offset, 1 - core, which, (way, which, step))
                ]
            drain(4)
    drain(0)
    for copy in sent:
        copy.wait_send()


def per_device(chips, test_feats, precond, train_feats, train_prob):
    tests, depth = test_feats.shape
    features = precond.shape[1]
    feats = features // (2 * chips)
    rows, half = tests // 2, chips // 2
    narrow = narrow_hops(chips)
    wide = half - narrow
    trains = train_feats.shape[0]
    dma = pltpu.SemaphoreType.DMA
    raw_scores = pl.pallas_call(
        functools.partial(kernel, chips, chips <= 8, narrow),
        out_shape=jax.ShapeDtypeStruct((trains, tests), F32),
        in_specs=[
            pl.BlockSpec(memory_space=pltpu.VMEM),
            pl.BlockSpec(memory_space=pl.ANY),
            pl.BlockSpec(memory_space=pl.ANY),
        ],
        out_specs=pl.BlockSpec(memory_space=pltpu.VMEM),
        scratch_shapes=[
            pltpu.VMEM((tests, depth), BF16),
            pltpu.VMEM((chips, depth, feats), BF16),
            pltpu.VMEM((chips, depth, feats), BF16),
            pltpu.VMEM((trains, features), BF16),
            pltpu.VMEM((2, tests, feats), F32),
            pltpu.VMEM((tests, feats), F32),
            pltpu.VMEM((2, 2, narrow + 1, rows, feats), BF16),
            pltpu.VMEM((2, 2, wide, rows, feats), F32),
            pltpu.VMEM((2, 2, narrow + 1, rows, feats), BF16),
            pltpu.VMEM((2, 2, wide, rows, feats), F32),
            pltpu.VMEM((2 * chips, tests, feats), BF16),
            dma((2, 1)),
            dma((chips,)),
            dma((2, chips)),
            dma,
            dma((2, 2, 2, half)),
            dma((2, 2, 2, half)),
            dma((2, 2, 2, half + 1)),
        ],
        compiler_params=pltpu.CompilerParams(
            collective_id=0, has_side_effects=True, vmem_limit_bytes=56 * 2**20
        ),
        cost_estimate=pl.CostEstimate(
            flops=4 * tests * depth * features + 2 * trains * tests * features,
            bytes_accessed=2 * (depth + trains) * features + 4 * trains * tests,
            transcendentals=0,
        ),
    )(test_feats, precond, train_feats)
    return raw_scores * (1.0 - train_prob)[:, None]


def solution(mesh):
    return jax.shard_map(
        functools.partial(per_device, mesh.shape["dp"] // 2),
        mesh=mesh,
        in_specs=(P("groups", "dp"), P("dp", None), P(("groups", "dp"), None), P(("groups", "dp"))),
        out_specs=P(("groups", "dp"), None),
        check_vma=False,
    )
```

```python
import functools

import jax
import jax.numpy as jnp
from jax import lax
from jax.experimental import pallas as pl
from jax.experimental.pallas import tpu as pltpu
from jax.sharding import PartitionSpec as P

MESH = pl.DeviceIdType.MESH
SUBS = 2
AHEAD = 3
F32, BF16 = jnp.float32, jnp.bfloat16


def narrow_hops(chips):
    count = 0
    while (count + 1) * (count + 2) <= 0.8 * chips and count + 1 < chips // 2:
        count += 1
    return count


def kernel(
    chips, folded, narrow,
    test_ref, precond_hbm, train_hbm, out_ref,
    test_other, own_p, other_p, train, part, mine,
    send16, send32, recv16, recv32, gathered,
    test_sems, own_sems, other_sems, train_sem,
    ring_sems, spread_sems, pair_sems,
):
    half = chips // 2
    tests, depth = test_ref.shape
    rows = tests // 2
    piece = rows // SUBS
    feats = own_p.shape[2]
    index = lax.axis_index("dp")
    core = index % 2
    chip = index // 2
    if folded:
        pos = chip // 2 + (chip % 2) * (chips - 1 - 2 * (chip // 2))
    else:
        pos = chip

    def device(place):
        place = (place + chips) % chips
        if folded:
            side = place // half
            place = 2 * (place + side * (chips - 1 - 2 * place)) + side
        return {"dp": place * 2 + core}

    pair = {"dp": chip * 2 + 1 - core}
    towards = (device(pos + 1), device(pos - 1))

    def columns(offset, which):
        block = ((pos + offset + chips) % chips) * 2 + which
        return pl.ds(pl.multiple_of(block * feats, feats), feats)

    order = [half]
    for distance in range(half - 1, 0, -1):
        order += [distance, -distance]
    order.append(0)

    barrier = pltpu.get_barrier_semaphore()
    train_copy = pltpu.make_async_copy(train_hbm, train, train_sem)
    own_copies = [
        pltpu.make_async_copy(
            precond_hbm.at[:, columns(offset, core)], own_p.at[at], own_sems.at[at]
        )
        for at, offset in enumerate(order)
    ]
    for copy in own_copies[:AHEAD]:
        copy.start()
    for other in (pair, *towards):
        pl.semaphore_signal(barrier, inc=1, device_id=other, device_id_type=MESH)
    pl.semaphore_wait(barrier, 3)

    def remote(src, dst, sems, where):
        return pltpu.make_async_remote_copy(
            src_ref=src, dst_ref=dst,
            send_sem=sems.at[(0, *where)], recv_sem=sems.at[(1, *where)],
            device_id=where_to[0], device_id_type=MESH,
        )

    where_to = [pair]
    sent = []
    test_copy = remote(test_ref, test_other, test_sems, (0,))
    test_copy.start()
    sent.append(test_copy)
    other_copies = []
    for at, offset in enumerate(order):
        copy = remote(
            precond_hbm.at[:, columns(offset, 1 - core)], other_p.at[at], other_sems, (at,)
        )
        sent.append(copy)
        other_copies.append(copy)
    for copy in other_copies[:AHEAD]:
        copy.start()

    tile = min(rows, 256)

    def partial_sum(offset, target):
        at = order.index(offset)
        own_copies[at].wait()
        if at == 0:
            test_copy.wait_recv()
        other_copies[at].wait_recv()

        @pl.loop(0, tests // tile)
        def _(step):
            here = pl.ds(pl.multiple_of(step * tile, tile), tile)
            target[here, :] = jnp.dot(
                test_ref[here, :], own_p[at], preferred_element_type=F32
            ) + jnp.dot(test_other[here, :], other_p[at], preferred_element_type=F32)

    def slot(way, part_at, step):
        count = step + 1 if way == part_at // SUBS else step
        if count <= narrow:
            return send16.at[way, part_at, step], recv16.at[way, part_at, step]
        return send32.at[way, part_at, step - narrow], recv32.at[way, part_at, step - narrow]

    def span(part_at):
        return pl.ds(part_at * piece, piece)

    ring = {}
    sign = (1, -1)
    partial_sum(half, part.at[0])
    for step in range(half):
        if step > 0:
            for way in (0, 1):
                partial_sum(sign[way] * (half - step), part.at[way])
        for leg in (0,) if step == 0 else (1, 0):
            for sub in range(SUBS):
                for way in (0, 1):
                    at = (way if leg == 0 else 1 - way) * SUBS + sub
                    source, target = slot(way, at, step)
                    value = part[0 if step == 0 else way, span(at), :]
                    if (way, at, step - 1) in ring:
                        ring[way, at, step - 1].wait_recv()
                        value = value + slot(way, at, step - 1)[1][...].astype(F32)
                    source[...] = value.astype(source.dtype)
                    where_to[0] = towards[way]
                    copy = remote(source, target, ring_sems, (way, at, step))
                    copy.start()
                    sent.append(copy)
                    ring[way, at, step] = copy
        if step == 0:
            for copy in own_copies[AHEAD:] + other_copies[AHEAD:]:
                copy.start()
            out_ref[...] = jnp.zeros_like(out_ref)
        if step == min(1, half - 1):
            train_copy.start()
    partial_sum(0, mine)

    def place(offset, which):
        return ((pos + offset + chips) % chips) * 2 + which

    spread, paired = {}, {}

    def forward(way, which, step):
        block = gathered.at[place(-sign[way] * step, core), span(which)]
        where_to[0] = towards[way]
        copy = remote(block, block, spread_sems, (way, which, step))
        copy.start()
        sent.append(copy)
        spread[way, which, step] = copy

    def hand_over(way, which, step):
        block = gathered.at[place(-sign[way] * step, core), span(which)]
        where_to[0] = pair
        copy = remote(block, block, pair_sems, (way, which, step))
        copy.start()
        sent.append(copy)
        paired[way, which, step] = copy

    def fold(offset, owner, which):
        block = place(offset, owner)
        cols = pl.ds(pl.multiple_of(block * feats, feats), feats)
        size = min(256, out_ref.shape[0])

        @pl.loop(0, out_ref.shape[0] // size)
        def _(step):
            here = pl.ds(pl.multiple_of(step * size, size), size)
            out_ref[here, which * rows:(which + 1) * rows] += lax.dot_general(
                train[here, cols], gathered[block, pl.ds(which * rows, rows), :],
                (((1,), (1,)), ((), ())), preferred_element_type=F32,
            )

    train_copy.wait()
    ready = []
    parts = [which * SUBS + sub for sub in range(SUBS) for which in (0, 1)]

    def arrived(offset, way, at, step):
        which, sub = at // SUBS, at % SUBS
        if sub == SUBS - 1:
            keys = [(way, which * SUBS + k, step) for k in range(SUBS)]
            ready.extend([(offset, core, which, []), (offset, 1 - core, which, keys)])

    for at in parts:
        total = mine[span(at), :]
        for way in (0, 1):
            ring[way, at, half - 1].wait_recv()
            total = total + slot(way, at, half - 1)[1][...].astype(F32)
        gathered[place(0, core), span(at), :] = total.astype(BF16)
        for way in (0, 1):
            if half > 1 or way == at // SUBS:
                forward(way, at, 0)
        hand_over(0, at, 0)
        arrived(0, 0, at, 0)

    def drain(limit):
        while len(ready) > limit:
            offset, owner, which, keys = ready.pop(0)
            for key in keys:
                paired[key].wait_recv()
            fold(offset, owner, which)

    for step in range(1, half + 1):
        for at in parts:
            for way in (0, 1):
                if (way, at, step - 1) not in spread:
                    continue
                spread[way, at, step - 1].wait_recv()
                if step < half and (step + 1 < half or way == at // SUBS):
                    forward(way, at, step)
                hand_over(way, at, step)
                arrived(-sign[way] * step, way, at, step)
            drain(4)
    drain(0)
    for copy in sent:
        copy.wait_send()


def per_device(chips, test_feats, precond, train_feats, train_prob):
    tests, depth = test_feats.shape
    features = precond.shape[1]
    feats = features // (2 * chips)
    pieces, half = 2 * SUBS, chips // 2
    piece = tests // pieces
    narrow = narrow_hops(chips)
    wide = half - narrow
    trains = train_feats.shape[0]
    dma = pltpu.SemaphoreType.DMA
    raw_scores = pl.pallas_call(
        functools.partial(kernel, chips, chips <= 8, narrow),
        out_shape=jax.ShapeDtypeStruct((trains, tests), F32),
        in_specs=[
            pl.BlockSpec(memory_space=pltpu.VMEM),
            pl.BlockSpec(memory_space=pl.ANY),
            pl.BlockSpec(memory_space=pl.ANY),
        ],
        out_specs=pl.BlockSpec(memory_space=pltpu.VMEM),
        scratch_shapes=[
            pltpu.VMEM((tests, depth), BF16),
            pltpu.VMEM((chips, depth, feats), BF16),
            pltpu.VMEM((chips, depth, feats), BF16),
            pltpu.VMEM((trains, features), BF16),
            pltpu.VMEM((2, tests, feats), F32),
            pltpu.VMEM((tests, feats), F32),
            pltpu.VMEM((2, pieces, narrow + 1, piece, feats), BF16),
            pltpu.VMEM((2, pieces, wide, piece, feats), F32),
            pltpu.VMEM((2, pieces, narrow + 1, piece, feats), BF16),
            pltpu.VMEM((2, pieces, wide, piece, feats), F32),
            pltpu.VMEM((2 * chips, tests, feats), BF16),
            dma((2, 1)),
            dma((chips,)),
            dma((2, chips)),
            dma,
            dma((2, 2, pieces, half)),
            dma((2, 2, pieces, half)),
            dma((2, 2, pieces, half + 1)),
        ],
        compiler_params=pltpu.CompilerParams(
            collective_id=0, has_side_effects=True, vmem_limit_bytes=56 * 2**20
        ),
        cost_estimate=pl.CostEstimate(
            flops=4 * tests * depth * features + 2 * trains * tests * features,
            bytes_accessed=2 * (depth + trains) * features + 4 * trains * tests,
            transcendentals=0,
        ),
    )(test_feats, precond, train_feats)
    return raw_scores * (1.0 - train_prob)[:, None]


def solution(mesh):
    return jax.shard_map(
        functools.partial(per_device, mesh.shape["dp"] // 2),
        mesh=mesh,
        in_specs=(P("groups", "dp"), P("dp", None), P(("groups", "dp"), None), P(("groups", "dp"))),
        out_specs=P(("groups", "dp"), None),
        check_vma=False,
    )
```

```python
import functools

import jax
import jax.numpy as jnp
from jax import lax
from jax.experimental import pallas as pl
from jax.experimental.pallas import tpu as pltpu
from jax.sharding import PartitionSpec as P

MESH = pl.DeviceIdType.MESH
SUBS = 2
AHEAD = 3
F32, BF16 = jnp.float32, jnp.bfloat16


def narrow_hops(chips):
    count = 0
    while (count + 2) ** 2 <= 1.125 * chips and count + 1 < chips // 2:
        count += 1
    return count


def kernel(
    chips, folded, narrow,
    test_ref, precond_hbm, train_hbm, out_ref,
    test_other, own_p, other_p, train, part, mine,
    send16, send32, recv16, recv32, gathered,
    test_sems, own_sems, other_sems, train_sem,
    ring_sems, spread_sems, pair_sems,
):
    half = chips // 2
    tests, depth = test_ref.shape
    rows = tests // 2
    piece = rows // SUBS
    feats = own_p.shape[2]
    index = lax.axis_index("dp")
    core = index % 2
    chip = index // 2
    if folded:
        pos = chip // 2 + (chip % 2) * (chips - 1 - 2 * (chip // 2))
    else:
        pos = chip

    def device(place):
        place = (place + chips) % chips
        if folded:
            side = place // half
            place = 2 * (place + side * (chips - 1 - 2 * place)) + side
        return {"dp": place * 2 + core}

    pair = {"dp": chip * 2 + 1 - core}
    towards = (device(pos + 1), device(pos - 1))

    def columns(offset, which):
        block = ((pos + offset + chips) % chips) * 2 + which
        return pl.ds(pl.multiple_of(block * feats, feats), feats)

    order = [half]
    for distance in range(half - 1, 0, -1):
        order += [distance, -distance]
    order.append(0)

    barrier = pltpu.get_barrier_semaphore()
    train_copy = pltpu.make_async_copy(train_hbm, train, train_sem)
    own_copies = [
        pltpu.make_async_copy(
            precond_hbm.at[:, columns(offset, core)], own_p.at[at], own_sems.at[at]
        )
        for at, offset in enumerate(order)
    ]
    for copy in own_copies[:AHEAD]:
        copy.start()
    for other in (pair, *towards):
        pl.semaphore_signal(barrier, inc=1, device_id=other, device_id_type=MESH)
    pl.semaphore_wait(barrier, 3)

    def remote(src, dst, sems, where):
        return pltpu.make_async_remote_copy(
            src_ref=src, dst_ref=dst,
            send_sem=sems.at[(0, *where)], recv_sem=sems.at[(1, *where)],
            device_id=where_to[0], device_id_type=MESH,
        )

    where_to = [pair]
    sent = []
    test_copy = remote(test_ref, test_other, test_sems, (0,))
    test_copy.start()
    sent.append(test_copy)
    other_copies = []
    for at, offset in enumerate(order):
        copy = remote(
            precond_hbm.at[:, columns(offset, 1 - core)], other_p.at[at], other_sems, (at,)
        )
        sent.append(copy)
        other_copies.append(copy)
    for copy in other_copies[:AHEAD]:
        copy.start()

    tile = min(rows, 256)

    def partial_sum(offset, target):
        at = order.index(offset)
        own_copies[at].wait()
        if at == 0:
            test_copy.wait_recv()
        other_copies[at].wait_recv()

        @pl.loop(0, tests // tile)
        def _(step):
            here = pl.ds(pl.multiple_of(step * tile, tile), tile)
            target[here, :] = jnp.dot(
                test_ref[here, :], own_p[at], preferred_element_type=F32
            ) + jnp.dot(test_other[here, :], other_p[at], preferred_element_type=F32)

    def slot(way, part_at, step):
        longer = way == part_at // SUBS
        if step < narrow if longer else step <= narrow + 1:
            return send16.at[way, part_at, step], recv16.at[way, part_at, step]
        return send32.at[way, part_at, step - narrow], recv32.at[way, part_at, step - narrow]

    def span(part_at):
        return pl.ds(part_at * piece, piece)

    ring = {}
    sign = (1, -1)
    partial_sum(half, part.at[0])
    for step in range(half):
        if step > 0:
            for way in (0, 1):
                partial_sum(sign[way] * (half - step), part.at[way])
        for leg in (0,) if step == 0 else (1, 0):
            for sub in range(SUBS):
                for way in (0, 1):
                    at = (way if leg == 0 else 1 - way) * SUBS + sub
                    source, target = slot(way, at, step)
                    value = part[0 if step == 0 else way, span(at), :]
                    if (way, at, step - 1) in ring:
                        ring[way, at, step - 1].wait_recv()
                        value = value + slot(way, at, step - 1)[1][...].astype(F32)
                    source[...] = value.astype(source.dtype)
                    where_to[0] = towards[way]
                    copy = remote(source, target, ring_sems, (way, at, step))
                    copy.start()
                    sent.append(copy)
                    ring[way, at, step] = copy
        if step == 0:
            for copy in own_copies[AHEAD:] + other_copies[AHEAD:]:
                copy.start()
            out_ref[...] = jnp.zeros_like(out_ref)
        if step == min(1, half - 1):
            train_copy.start()
    partial_sum(0, mine)

    def place(offset, which):
        return ((pos + offset + chips) % chips) * 2 + which

    spread, paired = {}, {}

    def forward(way, which, step):
        block = gathered.at[place(-sign[way] * step, core), span(which)]
        where_to[0] = towards[way]
        copy = remote(block, block, spread_sems, (way, which, step))
        copy.start()
        sent.append(copy)
        spread[way, which, step] = copy

    def hand_over(way, which, step):
        block = gathered.at[place(-sign[way] * step, core), span(which)]
        where_to[0] = pair
        copy = remote(block, block, pair_sems, (way, which, step))
        copy.start()
        sent.append(copy)
        paired[way, which, step] = copy

    def fold(offset, owner, which):
        block = place(offset, owner)
        cols = pl.ds(pl.multiple_of(block * feats, feats), feats)
        size = min(256, out_ref.shape[0])

        @pl.loop(0, out_ref.shape[0] // size)
        def _(step):
            here = pl.ds(pl.multiple_of(step * size, size), size)
            out_ref[here, which * rows:(which + 1) * rows] += lax.dot_general(
                train[here, cols], gathered[block, pl.ds(which * rows, rows), :],
                (((1,), (1,)), ((), ())), preferred_element_type=F32,
            )

    train_copy.wait()
    ready = []
    parts = [which * SUBS + sub for sub in range(SUBS) for which in (0, 1)]

    def arrived(offset, way, at, step):
        which, sub = at // SUBS, at % SUBS
        if sub == SUBS - 1:
            keys = [(way, which * SUBS + k, step) for k in range(SUBS)]
            ready.extend([(offset, core, which, []), (offset, 1 - core, which, keys)])

    for at in parts:
        total = mine[span(at), :]
        for way in (0, 1):
            ring[way, at, half - 1].wait_recv()
            total = total + slot(way, at, half - 1)[1][...].astype(F32)
        gathered[place(0, core), span(at), :] = total.astype(BF16)
        for way in (0, 1):
            if half > 1 or way == at // SUBS:
                forward(way, at, 0)
        hand_over(0, at, 0)
        arrived(0, 0, at, 0)

    def drain(limit):
        while len(ready) > limit:
            offset, owner, which, keys = ready.pop(0)
            for key in keys:
                paired[key].wait_recv()
            fold(offset, owner, which)

    for step in range(1, half + 1):
        for at in parts:
            for way in (0, 1):
                if (way, at, step - 1) not in spread:
                    continue
                spread[way, at, step - 1].wait_recv()
                if step < half and (step + 1 < half or way == at // SUBS):
                    forward(way, at, step)
                hand_over(way, at, step)
                arrived(-sign[way] * step, way, at, step)
            drain(4)
    drain(0)
    for copy in sent:
        copy.wait_send()


def per_device(chips, test_feats, precond, train_feats, train_prob):
    tests, depth = test_feats.shape
    features = precond.shape[1]
    feats = features // (2 * chips)
    pieces, half = 2 * SUBS, chips // 2
    piece = tests // pieces
    narrow = narrow_hops(chips)
    wide = half - narrow
    trains = train_feats.shape[0]
    dma = pltpu.SemaphoreType.DMA
    raw_scores = pl.pallas_call(
        functools.partial(kernel, chips, chips <= 8, narrow),
        out_shape=jax.ShapeDtypeStruct((trains, tests), F32),
        in_specs=[
            pl.BlockSpec(memory_space=pltpu.VMEM),
            pl.BlockSpec(memory_space=pl.ANY),
            pl.BlockSpec(memory_space=pl.ANY),
        ],
        out_specs=pl.BlockSpec(memory_space=pltpu.VMEM),
        scratch_shapes=[
            pltpu.VMEM((tests, depth), BF16),
            pltpu.VMEM((chips, depth, feats), BF16),
            pltpu.VMEM((chips, depth, feats), BF16),
            pltpu.VMEM((trains, features), BF16),
            pltpu.VMEM((2, tests, feats), F32),
            pltpu.VMEM((tests, feats), F32),
            pltpu.VMEM((2, pieces, narrow + 2, piece, feats), BF16),
            pltpu.VMEM((2, pieces, wide, piece, feats), F32),
            pltpu.VMEM((2, pieces, narrow + 2, piece, feats), BF16),
            pltpu.VMEM((2, pieces, wide, piece, feats), F32),
            pltpu.VMEM((2 * chips, tests, feats), BF16),
            dma((2, 1)),
            dma((chips,)),
            dma((2, chips)),
            dma,
            dma((2, 2, pieces, half)),
            dma((2, 2, pieces, half)),
            dma((2, 2, pieces, half + 1)),
        ],
        compiler_params=pltpu.CompilerParams(
            collective_id=0, has_side_effects=True, vmem_limit_bytes=56 * 2**20
        ),
        cost_estimate=pl.CostEstimate(
            flops=4 * tests * depth * features + 2 * trains * tests * features,
            bytes_accessed=2 * (depth + trains) * features + 4 * trains * tests,
            transcendentals=0,
        ),
    )(test_feats, precond, train_feats)
    return raw_scores * (1.0 - train_prob)[:, None]


def solution(mesh):
    return jax.shard_map(
        functools.partial(per_device, mesh.shape["dp"] // 2),
        mesh=mesh,
        in_specs=(P("groups", "dp"), P("dp", None), P(("groups", "dp"), None), P(("groups", "dp"))),
        out_specs=P(("groups", "dp"), None),
        check_vma=False,
    )
```
